32 devices in a mesh: shot: 2 (over x), tile: 16 (over z, y, core).
Axes of the slice: x: 2, y: 2, z: 4, core: 2. Of those that a mesh axis runs over, the one named last changes fastest.
Arguments:
- source: bfloat16 [16, 512, 4, 384], P('shot', 'tile'), parts along dimension 0, may hold values from -6 to 6
- receiver: bfloat16 [16, 512, 4, 384], P('shot', 'tile'), parts along dimension 0, may hold values from -6 to 6
- offsets: int32 [64], replicated, may hold values from -32 to 32, as said below
- snap_index: int32 [4], replicated, may hold values from 0 to 7, as said below
Outputs:
- image_lags: float32 [128, 512, 4, 384], P('shot', 'tile'), parts along dimension 0
The draws below stay inside these ranges and needn't reach their ends.
There are 2 independent parts, one for each index of `shot`. The reference program is written for one: setup_inputs(seed, part) draws one part's arguments, and reference() takes and returns one part's arrays. A program takes and returns all parts, laid end to end along the dimension named above; an argument that names none is the same for every part. Nothing has to cross between parts.
Inputs may be any that keep to these rules, and one draw needn't show every extreme that they name: `offsets`: distinct values; the lags -32 and 32 are always present. `snap_index`: distinct values; snapshots 0 and 7 are always present.
All inputs are finite; a program needn't handle non-finite values.
Results may differ from the reference program's by a relative error of at most 0.0003.
Values may be sent and summed in bfloat16 or wider, within the bound.
A program may use at most 192 MiB of HBM per device.

```python
import jax
import jax.numpy as jnp
from jax import lax

CY = 4
NZ = 384
NLAG = 64
HMAX = 32
NSTORE = 8
NUSE = 4
NX = 512


def draw_offsets(key, part):
    key_one, key_two = jax.random.split(jax.random.fold_in(key, 11))
    interior = jax.random.permutation(key_one, 2 * HMAX - 1)[:NLAG - 2] - (HMAX - 1)
    complete = jnp.concatenate([interior.astype(jnp.int32), jnp.array([-HMAX, HMAX], jnp.int32)])
    return jax.random.permutation(key_two, complete).astype(jnp.int32)


def draw_snap_index(key, part):
    key_one, key_two = jax.random.split(jax.random.fold_in(key, 23))
    interior = jax.random.permutation(key_one, NSTORE - 2)[:NUSE - 2] + 1
    complete = jnp.concatenate([interior.astype(jnp.int32), jnp.array([0, NSTORE - 1], jnp.int32)])
    return jax.random.permutation(key_two, complete).astype(jnp.int32)


def levels(rng, shape, cuts, low, high):
    def one(position, shards_of):
        steps = jax.random.uniform(jax.random.fold_in(jax.random.fold_in(rng, 6), position), (shards_of,), jnp.float32, low / len(cuts), high / len(cuts))
        return jnp.repeat(jnp.exp(steps), shape[position] // shards_of).reshape((-1,) + (1,) * (len(shape) - position - 1))

    gain = one(*cuts[0])
    for cut in cuts[1:]:
        gain = gain * one(*cut)
    return gain


def noise(key, extent, scale, reach, pieces=(), dtype=jnp.bfloat16):
    values = jax.random.normal(key, extent, jnp.float32) * scale
    if len(pieces) > 0:
        values = levels(key, extent, pieces, -0.22, 0.18) * values
    return jnp.clip(values, min=-reach, max=reach).astype(dtype)


def setup_inputs(seed: int = 0, part: int = 0) -> dict:
    splits = jax.random.split(jax.random.key(seed), 5)
    own_keys = jax.random.split(jax.random.fold_in(splits[4], part), 5)
    return {
        "source": noise(own_keys[0], (NSTORE, NX, CY, NZ), 1.0, 6.0, ((1, 16),)),
        "receiver": noise(own_keys[1], (NSTORE, NX, CY, NZ), 1.0, 6.0, ((1, 16),)),
        "offsets": draw_offsets(jax.random.fold_in(splits[4], 71), part),
        "snap_index": draw_snap_index(jax.random.fold_in(splits[4], 71), part),
    }


def reference(source, receiver, offsets, snap_index):
    source_sel = jnp.take(source, snap_index, axis=0)
    receiver_sel = jnp.take(receiver, snap_index, axis=0)
    padding = ((0, 0), (HMAX, HMAX), (0, 0), (0, 0))
    source_sel = jnp.pad(source_sel, padding)
    receiver_sel = jnp.pad(receiver_sel, padding)
    weights = (jnp.arange(NUSE).astype(jnp.float32) + 1.0) / NUSE

    def per_offset(offset):
        left_start = (HMAX - offset).astype(jnp.int32)
        right_start = (HMAX + offset).astype(jnp.int32)
        shifted_src = lax.dynamic_slice_in_dim(source_sel, left_start, NX, 1)
        shifted_rec = lax.dynamic_slice_in_dim(receiver_sel, right_start, NX, 1)
        product = shifted_src.astype(jnp.float32) * shifted_rec.astype(jnp.float32)
        return jnp.sum(product * weights[:, None, None, None], axis=0)

    return lax.map(per_offset, offsets)
```

```python
import functools

import jax
import jax.numpy as jnp
from jax import lax
from jax.experimental import pallas as pl
from jax.experimental.pallas import tpu as pltpu
from jax.sharding import PartitionSpec as P

HMAX = 32
LANES = 128
SUB = 8
MESH = pl.DeviceIdType.MESH


def exchange_kernel(tiles, used, snap_ref, src_ref, rec_ref, left_ref, right_ref, picked, send_sem, recv_sem):
    me = lax.axis_index("tile")
    has_left, has_right = me > 0, me < tiles - 1
    barrier = pltpu.get_barrier_semaphore()

    @pl.when(has_left)
    def _():
        pl.semaphore_signal(barrier, inc=1, device_id={"tile": me - 1}, device_id_type=MESH)

    @pl.when(has_right)
    def _():
        pl.semaphore_signal(barrier, inc=1, device_id={"tile": me + 1}, device_id_type=MESH)

    def up(snap):
        return pltpu.make_async_remote_copy(
            src_ref=picked.at[snap],
            dst_ref=left_ref.at[snap],
            send_sem=send_sem.at[0, snap],
            recv_sem=recv_sem.at[0, snap],
            device_id={"tile": me + 1},
            device_id_type=MESH,
        )

    def down(snap):
        return pltpu.make_async_remote_copy(
            src_ref=picked.at[snap],
            dst_ref=right_ref.at[snap],
            send_sem=send_sem.at[1, snap],
            recv_sem=recv_sem.at[1, snap],
            device_id={"tile": me - 1},
            device_id_type=MESH,
        )

    for snap in range(used):
        picked[snap, 0] = src_ref[snap_ref[snap]]
        picked[snap, 1] = rec_ref[snap_ref[snap]]
        if snap == 0:
            pl.semaphore_wait(barrier, has_left.astype(jnp.int32) + has_right.astype(jnp.int32))

        @pl.when(has_right)
        def _():
            up(snap).start()

        @pl.when(has_left)
        def _():
            down(snap).start()

    for snap in range(used):
        @pl.when(has_right)
        def _():
            up(snap).wait_send()
            down(snap).wait_recv()

        @pl.when(has_left)
        def _():
            down(snap).wait_send()
            up(snap).wait_recv()


def image_kernel(
    tiles, used, lags, cell_rows,
    offset_ref, snap_ref, src_ref, rec_ref, left_ref, right_ref, out_ref,
    raw, fields, image, slot_ref, in_sem, out_sem,
):
    me = lax.axis_index("tile")
    cells, cy, nz = src_ref.shape[1:]
    blocks = nz // LANES
    rows = cells * cell_rows
    pairs = cells // 2
    step = 2 * cell_rows
    base = HMAX * cell_rows

    def lanes(block):
        return pl.ds(block * LANES, LANES)

    own, sides = [], []
    for block in range(blocks):
        for snap in range(used):
            for field, ref in enumerate((src_ref, rec_ref)):
                own.append(pltpu.make_async_copy(
                    ref.at[snap_ref[snap], :, :, lanes(block)],
                    raw.at[1, snap, field, :, block], in_sem.at[1, block, snap, field]))
        for place, ref in ((0, left_ref), (2, right_ref)):
            sides.append(pltpu.make_async_copy(
                ref.at[:, :, :, :, lanes(block)], raw.at[place, :, :, :, block], in_sem.at[place, block, 0, 0]))
    for copy in own + sides:
        copy.start()

    for index in range(2 * HMAX + 1):
        slot_ref[index] = -1
    for lag in range(lags):
        slot_ref[offset_ref[lag] + HMAX] = lag

    def widen(place):
        def body(snap, carry):
            for field in range(2):
                value = raw.at[place, snap, field].reshape(rows, LANES)[...].astype(jnp.float32)
                if field == 0:
                    value = value * ((snap + 1).astype(jnp.float32) / used)
                fields[field, snap, pl.ds(place * rows, rows), :] = value
            return carry
        lax.fori_loop(0, used, body, 0)

    def clear(place):
        def body(snap, carry):
            for field in range(2):
                fields[field, snap, pl.ds(place * rows, rows), :] = jnp.zeros((rows, LANES), jnp.float32)
            return carry
        lax.fori_loop(0, used, body, 0)

    for copy in own:
        copy.wait()
    widen(1)
    for copy in sides:
        copy.wait()
    for place, edge in ((0, me == 0), (2, me == tiles - 1)):
        pl.when(edge)(functools.partial(clear, place))
        pl.when(jnp.logical_not(edge))(functools.partial(widen, place))

    def send(index, slot):
        for block in range(blocks):
            pltpu.make_async_copy(
                image.at[index, :, block], out_ref.at[slot, :, :, lanes(block)], out_sem).start()

    def group(first, odd, width):
        def one_class(part, carry):
            inner = part * SUB
            cache = {}

            def source(place):
                start = base + inner + step * (place - first) - cell_rows * odd
                start = pl.multiple_of(start, 4)
                return [fields[0, snap, pl.ds(start, SUB), :] for snap in range(used)]

            def receiver(place):
                if place not in cache:
                    start = base + inner + step * (place + first) + cell_rows * odd
                    start = pl.multiple_of(start, 4)
                    cache[place] = [fields[1, snap, pl.ds(start, SUB), :] for snap in range(used)]
                return cache[place]

            for place in range(-(width - 1), pairs):
                held = source(place)
                for late in range(width):
                    pair = place + late
                    if 0 <= pair < pairs:
                        other = receiver(place + 2 * late)
                        total = held[0] * other[0]
                        for snap in range(1, used):
                            total = total + held[snap] * other[snap]
                        index = 2 * (first + late) + odd + HMAX
                        sheet = image.at[index].reshape(rows, LANES)
                        sheet[pl.ds(pl.multiple_of(step * pair + inner, SUB), SUB), :] = total
            return carry

        lax.fori_loop(0, step // SUB, one_class, 0)
        for late in range(width):
            index = 2 * (first + late) + odd + HMAX
            slot = slot_ref[index]

            @pl.when(slot >= 0)
            def _():
                send(index, slot)

    def even_groups(number, carry):
        group(3 * number - HMAX // 2, 0, 3)
        return carry

    def odd_groups(number, carry):
        group(4 * number - HMAX // 2, 1, 4)
        return carry

    lax.fori_loop(0, (HMAX + 1) // 3, even_groups, 0)
    lax.fori_loop(0, HMAX // 4, odd_groups, 0)
    for block in range(blocks):
        pltpu.make_async_copy(
            image.at[pl.ds(0, lags), :, block], out_ref.at[:, :, :, lanes(block)], out_sem).wait()


def local(tiles, source, receiver, offsets, snap_index):
    stored, cells, cy, nz = source.shape
    used, lags = snap_index.shape[0], offsets.shape[0]
    cell_rows = cy * nz // LANES
    rows = cells * cell_rows
    assert cells == HMAX and (2 * cell_rows) % SUB == 0
    halo = jax.ShapeDtypeStruct((used, 2, cells, cy, nz), source.dtype)
    vmem = pl.BlockSpec(memory_space=pltpu.VMEM)
    smem = pl.BlockSpec(memory_space=pltpu.SMEM)
    anywhere = pl.BlockSpec(memory_space=pl.ANY)
    left, right = pl.pallas_call(
        functools.partial(exchange_kernel, tiles, used),
        out_shape=(halo, halo),
        in_specs=[smem, vmem, vmem],
        out_specs=(anywhere, anywhere),
        scratch_shapes=[
            pltpu.VMEM((used, 2, cells, cy, nz), source.dtype),
            pltpu.SemaphoreType.DMA((2, used)),
            pltpu.SemaphoreType.DMA((2, used)),
        ],
        compiler_params=pltpu.CompilerParams(
            collective_id=0, has_side_effects=True, vmem_limit_bytes=16 << 20),
    )(snap_index, source, receiver)
    return pl.pallas_call(
        functools.partial(image_kernel, tiles, used, lags, cell_rows),
        out_shape=jax.ShapeDtypeStruct((lags, cells, cy, nz), jnp.float32),
        in_specs=[smem, smem, anywhere, anywhere, anywhere, anywhere],
        out_specs=anywhere,
        scratch_shapes=[
            pltpu.VMEM((3, used, 2, cells, nz // LANES, cy, LANES), source.dtype),
            pltpu.VMEM((2, used, 3 * rows, LANES), jnp.float32),
            pltpu.VMEM((2 * HMAX + 1, cells, nz // LANES, cy, LANES), jnp.float32),
            pltpu.SMEM((2 * HMAX + 1,), jnp.int32),
            pltpu.SemaphoreType.DMA((3, nz // LANES, used, 2)),
            pltpu.SemaphoreType.DMA(()),
        ],
        compiler_params=pltpu.CompilerParams(vmem_limit_bytes=40 << 20),
    )(offsets, snap_index, source, receiver, left, right)


def solution(mesh):
    return jax.shard_map(
        functools.partial(local, mesh.shape["tile"]),
        mesh=mesh,
        in_specs=(P("shot", "tile", None, None), P("shot", "tile", None, None), P(), P()),
        out_specs=P("shot", "tile", None, None),
        check_vma=False,
    )
```

```python
import functools

import jax
import jax.numpy as jnp
from jax import lax
from jax.experimental import pallas as pl
from jax.experimental.pallas import tpu as pltpu
from jax.sharding import PartitionSpec as P

HMAX = 32
LANES = 128
SUB = 8
MESH = pl.DeviceIdType.MESH


def lag_group(fields, cell_rows, pairs, first, odd, width, put):
    step = 2 * cell_rows
    base = HMAX * cell_rows

    def one_class(part, carry):
        inner = part * SUB
        cache = {}

        def source(place):
            start = base + inner + step * (place - first) - cell_rows * odd
            return fields[0, pl.ds(pl.multiple_of(start, 4), SUB), :]

        def receiver(place):
            if place not in cache:
                start = base + inner + step * (place + first) + cell_rows * odd
                cache[place] = fields[1, pl.ds(pl.multiple_of(start, 4), SUB), :]
            return cache[place]

        for place in range(-(width - 1), pairs):
            held = source(place)
            for late in range(width):
                pair = place + late
                if 0 <= pair < pairs:
                    index = 2 * (first + late) + odd + HMAX
                    rows = pl.ds(pl.multiple_of(step * pair + inner, SUB), SUB)
                    put(index, rows, held * receiver(place + 2 * late))
        return carry

    lax.fori_loop(0, step // SUB, one_class, 0)


def exchange_kernel(
    tiles, used, cell_rows, snap_ref, src_ref, rec_ref, partial_ref, last_ref,
    stage, picked, halo, fields, in_sem, send_sem, recv_sem,
):
    me = lax.axis_index("tile")
    has_left, has_right = me > 0, me < tiles - 1
    stored, cells, cy, nz = src_ref.shape
    blocks = nz // LANES
    rows = cells * cell_rows
    barrier = pltpu.get_barrier_semaphore()

    @pl.when(has_left)
    def _():
        pl.semaphore_signal(barrier, inc=1, device_id={"tile": me - 1}, device_id_type=MESH)

    @pl.when(has_right)
    def _():
        pl.semaphore_signal(barrier, inc=1, device_id={"tile": me + 1}, device_id_type=MESH)

    loads = [
        pltpu.make_async_copy(
            ref.at[:, :, :, pl.ds(block * LANES, LANES)], stage.at[field, :, :, block], in_sem.at[field, block])
        for field, ref in enumerate((src_ref, rec_ref))
        for block in range(blocks)
    ]
    for copy in loads:
        copy.start()

    def up(snap):
        return pltpu.make_async_remote_copy(
            src_ref=picked.at[snap],
            dst_ref=halo.at[0, snap],
            send_sem=send_sem.at[0, snap],
            recv_sem=recv_sem.at[0, snap],
            device_id={"tile": me + 1},
            device_id_type=MESH,
        )

    def down(snap):
        return pltpu.make_async_remote_copy(
            src_ref=picked.at[snap],
            dst_ref=halo.at[1, snap],
            send_sem=send_sem.at[1, snap],
            recv_sem=recv_sem.at[1, snap],
            device_id={"tile": me - 1},
            device_id_type=MESH,
        )

    for copy in loads:
        copy.wait()
    rowwise = stage.reshape(2, stored, rows, LANES)
    for snap in range(used):
        for field in range(2):
            picked[snap, field] = rowwise[field, snap_ref[snap]]
        if snap == 0:
            pl.semaphore_wait(barrier, has_left.astype(jnp.int32) + has_right.astype(jnp.int32))

        @pl.when(has_right)
        def _():
            up(snap).start()

        @pl.when(has_left)
        def _():
            down(snap).start()

    def clear(place):
        for field in range(2):
            for ref in (fields, last_ref):
                ref[field, pl.ds(place * rows, rows), :] = jnp.zeros((rows, LANES), jnp.float32)

    pl.when(jnp.logical_not(has_left))(functools.partial(clear, 0))
    pl.when(jnp.logical_not(has_right))(functools.partial(clear, 2))

    def zero(index, carry):
        partial_ref[index] = jnp.zeros((rows, LANES), jnp.float32)
        return carry

    lax.fori_loop(0, 2 * HMAX + 1, zero, 0)

    def widen(target, place, value, field, snap):
        value = value.astype(jnp.float32)
        if field == 0:
            value = value * ((snap + 1).astype(jnp.float32) / used)
        target[field, pl.ds(place * rows, rows), :] = value

    def gather(target, snap):
        for field in range(2):
            widen(target, 1, picked[snap, field], field, snap)

        @pl.when(has_left)
        def _():
            up(snap).wait_recv()
            for field in range(2):
                widen(target, 0, halo[0, snap, field], field, snap)

        @pl.when(has_right)
        def _():
            down(snap).wait_recv()
            for field in range(2):
                widen(target, 2, halo[1, snap, field], field, snap)

    def put(index, where, term):
        partial_ref[index, where, :] += term

    def add(snap, carry):
        gather(fields, snap)

        def even_groups(number, inner):
            lag_group(fields, cell_rows, cells // 2, 11 * number - HMAX // 2, 0, 11, put)
            return inner

        def odd_groups(number, inner):
            lag_group(fields, cell_rows, cells // 2, 8 * number - HMAX // 2, 1, 8, put)
            return inner

        lax.fori_loop(0, (HMAX + 1) // 11, even_groups, 0)
        lax.fori_loop(0, HMAX // 8, odd_groups, 0)
        return carry

    lax.fori_loop(0, used - 1, add, 0)
    gather(last_ref, jnp.int32(used - 1))

    for snap in range(used):
        @pl.when(has_right)
        def _():
            up(snap).wait_send()

        @pl.when(has_left)
        def _():
            down(snap).wait_send()


def image_kernel(lags, cell_rows, offset_ref, partial_ref, last_ref, out_ref, image, slot_ref, out_sem):
    cells, cy, nz = out_ref.shape[1:]
    blocks = nz // LANES
    rows = cells * cell_rows

    for index in range(2 * HMAX + 1):
        slot_ref[index] = -1
    for lag in range(lags):
        slot_ref[offset_ref[lag] + HMAX] = lag

    def lanes(block):
        return pl.ds(block * LANES, LANES)

    def put(index, where, term):
        sheet = image.at[index].reshape(rows, LANES)
        sheet[where, :] = partial_ref[index, where, :] + term

    def group(first, odd, width):
        lag_group(last_ref, cell_rows, cells // 2, first, odd, width, put)
        for late in range(width):
            index = 2 * (first + late) + odd + HMAX
            slot = slot_ref[index]

            @pl.when(slot >= 0)
            def _():
                for block in range(blocks):
                    pltpu.make_async_copy(
                        image.at[index, :, block], out_ref.at[slot, :, :, lanes(block)], out_sem).start()

    def even_groups(number, carry):
        group(3 * number - HMAX // 2, 0, 3)
        return carry

    def odd_groups(number, carry):
        group(4 * number - HMAX // 2, 1, 4)
        return carry

    lax.fori_loop(0, (HMAX + 1) // 3, even_groups, 0)
    lax.fori_loop(0, HMAX // 4, odd_groups, 0)
    for block in range(blocks):
        pltpu.make_async_copy(
            image.at[pl.ds(0, lags), :, block], out_ref.at[:, :, :, lanes(block)], out_sem).wait()


def local(tiles, source, receiver, offsets, snap_index):
    stored, cells, cy, nz = source.shape
    used, lags = snap_index.shape[0], offsets.shape[0]
    blocks = nz // LANES
    cell_rows = cy * blocks
    rows = cells * cell_rows
    assert cells == HMAX and (2 * cell_rows) % SUB == 0
    vmem = pl.BlockSpec(memory_space=pltpu.VMEM)
    smem = pl.BlockSpec(memory_space=pltpu.SMEM)
    anywhere = pl.BlockSpec(memory_space=pl.ANY)
    every = 2 * HMAX + 1
    partial, last = pl.pallas_call(
        functools.partial(exchange_kernel, tiles, used, cell_rows),
        out_shape=(
            jax.ShapeDtypeStruct((every, rows, LANES), jnp.float32),
            jax.ShapeDtypeStruct((2, 3 * rows, LANES), jnp.float32),
        ),
        in_specs=[smem, anywhere, anywhere],
        out_specs=(vmem, vmem),
        scratch_shapes=[
            pltpu.VMEM((2, stored, cells, blocks, cy, LANES), source.dtype),
            pltpu.VMEM((used, 2, rows, LANES), source.dtype),
            pltpu.VMEM((2, used, 2, rows, LANES), source.dtype),
            pltpu.VMEM((2, 3 * rows, LANES), jnp.float32),
            pltpu.SemaphoreType.DMA((2, blocks)),
            pltpu.SemaphoreType.DMA((2, used)),
            pltpu.SemaphoreType.DMA((2, used)),
        ],
        compiler_params=pltpu.CompilerParams(
            collective_id=0, has_side_effects=True, vmem_limit_bytes=32 << 20),
    )(snap_index, source, receiver)
    return pl.pallas_call(
        functools.partial(image_kernel, lags, cell_rows),
        out_shape=jax.ShapeDtypeStruct((lags, cells, cy, nz), jnp.float32),
        in_specs=[smem, vmem, vmem],
        out_specs=anywhere,
        scratch_shapes=[
            pltpu.VMEM((every, cells, blocks, cy, LANES), jnp.float32),
            pltpu.SMEM((every,), jnp.int32),
            pltpu.SemaphoreType.DMA(()),
        ],
        compiler_params=pltpu.CompilerParams(vmem_limit_bytes=32 << 20),
    )(offsets, partial, last)


def solution(mesh):
    return jax.shard_map(
        functools.partial(local, mesh.shape["tile"]),
        mesh=mesh,
        in_specs=(P("shot", "tile", None, None), P("shot", "tile", None, None), P(), P()),
        out_specs=P("shot", "tile", None, None),
        check_vma=False,
    )
```

```python
import functools

import jax
import jax.numpy as jnp
from jax import lax
from jax.experimental import pallas as pl
from jax.experimental.pallas import tpu as pltpu
from jax.sharding import PartitionSpec as P

HMAX = 32
LANES = 128
SUB = 8
MESH = pl.DeviceIdType.MESH


def lag_group(fields, cell_rows, pairs, first, odd, width, put):
    step = 2 * cell_rows
    base = HMAX * cell_rows

    def one_class(part, carry):
        inner = part * SUB
        cache = {}

        def source(place):
            start = base + inner + step * (place - first) - cell_rows * odd
            return fields[0, pl.ds(pl.multiple_of(start, 4), SUB), :]

        def receiver(place):
            if place not in cache:
                start = base + inner + step * (place + first) + cell_rows * odd
                cache[place] = fields[1, pl.ds(pl.multiple_of(start, 4), SUB), :]
            return cache[place]

        for place in range(-(width - 1), pairs):
            held = source(place)
            for late in range(width):
                pair = place + late
                if 0 <= pair < pairs:
                    index = 2 * (first + late) + odd + HMAX
                    rows = pl.ds(pl.multiple_of(step * pair + inner, SUB), SUB)
                    put(index, rows, held * receiver(place + 2 * late))
        return carry

    lax.fori_loop(0, step // SUB, one_class, 0)


def pick_kernel(used, snap_ref, src_ref, rec_ref, picked_ref, sem):
    blocks = src_ref.shape[3] // LANES
    copies = [
        pltpu.make_async_copy(
            ref.at[snap_ref[snap], :, :, pl.ds(block * LANES, LANES)],
            picked_ref.at[snap, field, :, block], sem.at[snap, field, block])
        for snap in range(used)
        for field, ref in enumerate((src_ref, rec_ref))
        for block in range(blocks)
    ]
    for copy in copies:
        copy.start()
    for copy in copies:
        copy.wait()


def exchange_kernel(
    tiles, cell_rows, picked, partial_ref, last_ref, halo, fields, send_sem, recv_sem,
):
    me = lax.axis_index("tile")
    has_left, has_right = me > 0, me < tiles - 1
    used, _, cells, blocks, cy, _ = picked.shape
    rows = cells * cell_rows
    barrier = pltpu.get_barrier_semaphore()

    @pl.when(has_left)
    def _():
        pl.semaphore_signal(barrier, inc=1, device_id={"tile": me - 1}, device_id_type=MESH)

    @pl.when(has_right)
    def _():
        pl.semaphore_signal(barrier, inc=1, device_id={"tile": me + 1}, device_id_type=MESH)

    def up(snap):
        return pltpu.make_async_remote_copy(
            src_ref=picked.at[snap],
            dst_ref=halo.at[0, snap],
            send_sem=send_sem.at[0, snap],
            recv_sem=recv_sem.at[0, snap],
            device_id={"tile": me + 1},
            device_id_type=MESH,
        )

    def down(snap):
        return pltpu.make_async_remote_copy(
            src_ref=picked.at[snap],
            dst_ref=halo.at[1, snap],
            send_sem=send_sem.at[1, snap],
            recv_sem=recv_sem.at[1, snap],
            device_id={"tile": me - 1},
            device_id_type=MESH,
        )

    beside = halo.reshape(2, used, 2, rows, LANES)
    own = picked.reshape(used, 2, rows, LANES)
    pl.semaphore_wait(barrier, has_left.astype(jnp.int32) + has_right.astype(jnp.int32))
    for snap in range(used):
        @pl.when(has_right)
        def _():
            up(snap).start()

        @pl.when(has_left)
        def _():
            down(snap).start()

    def clear(place):
        for field in range(2):
            for ref in (fields, last_ref):
                ref[field, pl.ds(place * rows, rows), :] = jnp.zeros((rows, LANES), jnp.float32)

    pl.when(jnp.logical_not(has_left))(functools.partial(clear, 0))
    pl.when(jnp.logical_not(has_right))(functools.partial(clear, 2))

    def zero(index, carry):
        partial_ref[index] = jnp.zeros((rows, LANES), jnp.float32)
        return carry

    lax.fori_loop(0, 2 * HMAX + 1, zero, 0)

    def widen(target, place, value, field, snap):
        value = value.astype(jnp.float32)
        if field == 0:
            value = value * ((snap + 1).astype(jnp.float32) / used)
        target[field, pl.ds(place * rows, rows), :] = value

    def gather(target, snap):
        for field in range(2):
            widen(target, 1, own[snap, field], field, snap)

        @pl.when(has_left)
        def _():
            up(snap).wait_recv()
            for field in range(2):
                widen(target, 0, beside[0, snap, field], field, snap)

        @pl.when(has_right)
        def _():
            down(snap).wait_recv()
            for field in range(2):
                widen(target, 2, beside[1, snap, field], field, snap)

    def put(index, where, term):
        partial_ref[index, where, :] += term

    def add(snap, carry):
        gather(fields, snap)

        def even_groups(number, inner):
            lag_group(fields, cell_rows, cells // 2, 11 * number - HMAX // 2, 0, 11, put)
            return inner

        def odd_groups(number, inner):
            lag_group(fields, cell_rows, cells // 2, 8 * number - HMAX // 2, 1, 8, put)
            return inner

        lax.fori_loop(0, (HMAX + 1) // 11, even_groups, 0)
        lax.fori_loop(0, HMAX // 8, odd_groups, 0)
        return carry

    lax.fori_loop(0, used - 1, add, 0)
    gather(last_ref, jnp.int32(used - 1))

    for snap in range(used):
        @pl.when(has_right)
        def _():
            up(snap).wait_send()

        @pl.when(has_left)
        def _():
            down(snap).wait_send()


def image_kernel(lags, cell_rows, offset_ref, partial_ref, last_ref, out_ref, image, slot_ref, out_sem):
    cells, cy, nz = out_ref.shape[1:]
    blocks = nz // LANES
    rows = cells * cell_rows

    for index in range(2 * HMAX + 1):
        slot_ref[index] = -1
    for lag in range(lags):
        slot_ref[offset_ref[lag] + HMAX] = lag

    def lanes(block):
        return pl.ds(block * LANES, LANES)

    def put(index, where, term):
        sheet = image.at[index].reshape(rows, LANES)
        sheet[where, :] = partial_ref[index, where, :] + term

    def group(first, odd, width):
        lag_group(last_ref, cell_rows, cells // 2, first, odd, width, put)
        for late in range(width):
            index = 2 * (first + late) + odd + HMAX
            slot = slot_ref[index]

            @pl.when(slot >= 0)
            def _():
                for block in range(blocks):
                    pltpu.make_async_copy(
                        image.at[index, :, block], out_ref.at[slot, :, :, lanes(block)], out_sem).start()

    def even_groups(number, carry):
        group(3 * number - HMAX // 2, 0, 3)
        return carry

    def odd_groups(number, carry):
        group(4 * number - HMAX // 2, 1, 4)
        return carry

    lax.fori_loop(0, (HMAX + 1) // 3, even_groups, 0)
    lax.fori_loop(0, HMAX // 4, odd_groups, 0)
    for block in range(blocks):
        pltpu.make_async_copy(
            image.at[pl.ds(0, lags), :, block], out_ref.at[:, :, :, lanes(block)], out_sem).wait()


def local(tiles, source, receiver, offsets, snap_index):
    stored, cells, cy, nz = source.shape
    used, lags = snap_index.shape[0], offsets.shape[0]
    blocks = nz // LANES
    cell_rows = cy * blocks
    rows = cells * cell_rows
    assert cells == HMAX and (2 * cell_rows) % SUB == 0
    vmem = pl.BlockSpec(memory_space=pltpu.VMEM)
    smem = pl.BlockSpec(memory_space=pltpu.SMEM)
    anywhere = pl.BlockSpec(memory_space=pl.ANY)
    every = 2 * HMAX + 1
    picked = pl.pallas_call(
        functools.partial(pick_kernel, used),
        out_shape=jax.ShapeDtypeStruct((used, 2, cells, blocks, cy, LANES), source.dtype),
        in_specs=[smem, anywhere, anywhere],
        out_specs=vmem,
        scratch_shapes=[pltpu.SemaphoreType.DMA((used, 2, blocks))],
        compiler_params=pltpu.CompilerParams(vmem_limit_bytes=62 << 20),
    )(snap_index, source, receiver)
    partial, last = pl.pallas_call(
        functools.partial(exchange_kernel, tiles, cell_rows),
        out_shape=(
            jax.ShapeDtypeStruct((every, rows, LANES), jnp.float32),
            jax.ShapeDtypeStruct((2, 3 * rows, LANES), jnp.float32),
        ),
        in_specs=[vmem],
        out_specs=(vmem, vmem),
        scratch_shapes=[
            pltpu.VMEM((2, used, 2, cells, blocks, cy, LANES), source.dtype),
            pltpu.VMEM((2, 3 * rows, LANES), jnp.float32),
            pltpu.SemaphoreType.DMA((2, used)),
            pltpu.SemaphoreType.DMA((2, used)),
        ],
        compiler_params=pltpu.CompilerParams(
            collective_id=0, has_side_effects=True, vmem_limit_bytes=32 << 20),
    )(picked)
    return pl.pallas_call(
        functools.partial(image_kernel, lags, cell_rows),
        out_shape=jax.ShapeDtypeStruct((lags, cells, cy, nz), jnp.float32),
        in_specs=[smem, vmem, vmem],
        out_specs=anywhere,
        scratch_shapes=[
            pltpu.VMEM((every, cells, blocks, cy, LANES), jnp.float32),
            pltpu.SMEM((every,), jnp.int32),
            pltpu.SemaphoreType.DMA(()),
        ],
        compiler_params=pltpu.CompilerParams(vmem_limit_bytes=32 << 20),
    )(offsets, partial, last)


def solution(mesh):
    return jax.shard_map(
        functools.partial(local, mesh.shape["tile"]),
        mesh=mesh,
        in_specs=(P("shot", "tile", None, None), P("shot", "tile", None, None), P(), P()),
        out_specs=P("shot", "tile", None, None),
        check_vma=False,
    )
```

```python
import functools

import jax
import jax.numpy as jnp
from jax import lax
from jax.experimental import pallas as pl
from jax.experimental.pallas import tpu as pltpu
from jax.sharding import PartitionSpec as P

HMAX = 32
LANES = 128
SUB = 8
MESH = pl.DeviceIdType.MESH


def lag_group(fields, cell_rows, pairs, first, odd, width, put):
    step = 2 * cell_rows
    base = HMAX * cell_rows

    def one_class(part, carry):
        inner = part * SUB
        cache = {}

        def source(place):
            start = base + inner + step * (place - first) - cell_rows * odd
            return fields[0, pl.ds(pl.multiple_of(start, 4), SUB), :]

        def receiver(place):
            if place not in cache:
                start = base + inner + step * (place + first) + cell_rows * odd
                cache[place] = fields[1, pl.ds(pl.multiple_of(start, 4), SUB), :]
            return cache[place]

        for place in range(-(width - 1), pairs):
            held = source(place)
            for late in range(width):
                pair = place + late
                if 0 <= pair < pairs:
                    index = 2 * (first + late) + odd + HMAX
                    rows = pl.ds(pl.multiple_of(step * pair + inner, SUB), SUB)
                    put(index, rows, held * receiver(place + 2 * late))
        return carry

    lax.fori_loop(0, step // SUB, one_class, 0)


def exchange_kernel(
    tiles, cell_rows, snap_ref, src_ref, rec_ref, partial_ref, last_ref,
    picked, halo, fields, send_sem, recv_sem,
):
    me = lax.axis_index("tile")
    has_left, has_right = me > 0, me < tiles - 1
    used, _, cells, blocks, cy, _ = picked.shape
    rows = cells * cell_rows
    barrier = pltpu.get_barrier_semaphore()

    @pl.when(has_left)
    def _():
        pl.semaphore_signal(barrier, inc=1, device_id={"tile": me - 1}, device_id_type=MESH)

    @pl.when(has_right)
    def _():
        pl.semaphore_signal(barrier, inc=1, device_id={"tile": me + 1}, device_id_type=MESH)

    def up(snap):
        return pltpu.make_async_remote_copy(
            src_ref=picked.at[snap],
            dst_ref=halo.at[0, snap],
            send_sem=send_sem.at[0, snap],
            recv_sem=recv_sem.at[0, snap],
            device_id={"tile": me + 1},
            device_id_type=MESH,
        )

    def down(snap):
        return pltpu.make_async_remote_copy(
            src_ref=picked.at[snap],
            dst_ref=halo.at[1, snap],
            send_sem=send_sem.at[1, snap],
            recv_sem=recv_sem.at[1, snap],
            device_id={"tile": me - 1},
            device_id_type=MESH,
        )

    beside = halo.reshape(2, used, 2, rows, LANES)
    own = picked.reshape(used, 2, rows, LANES)
    for snap in range(used):
        for field, ref in enumerate((src_ref, rec_ref)):
            for block in range(blocks):
                picked[snap, field, :, block] = ref[snap_ref[snap], :, :, pl.ds(block * LANES, LANES)]
        if snap == 0:
            pl.semaphore_wait(barrier, has_left.astype(jnp.int32) + has_right.astype(jnp.int32))

        @pl.when(has_right)
        def _():
            up(snap).start()

        @pl.when(has_left)
        def _():
            down(snap).start()

    def clear(place):
        for field in range(2):
            for ref in (fields, last_ref):
                ref[field, pl.ds(place * rows, rows), :] = jnp.zeros((rows, LANES), jnp.float32)

    pl.when(jnp.logical_not(has_left))(functools.partial(clear, 0))
    pl.when(jnp.logical_not(has_right))(functools.partial(clear, 2))

    def zero(index, carry):
        partial_ref[index] = jnp.zeros((rows, LANES), jnp.float32)
        return carry

    lax.fori_loop(0, 2 * HMAX + 1, zero, 0)

    def widen(target, place, value, field, snap):
        value = value.astype(jnp.float32)
        if field == 0:
            value = value * ((snap + 1).astype(jnp.float32) / used)
        target[field, pl.ds(place * rows, rows), :] = value

    def gather(target, snap):
        for field in range(2):
            widen(target, 1, own[snap, field], field, snap)

        @pl.when(has_left)
        def _():
            up(snap).wait_recv()
            for field in range(2):
                widen(target, 0, beside[0, snap, field], field, snap)

        @pl.when(has_right)
        def _():
            down(snap).wait_recv()
            for field in range(2):
                widen(target, 2, beside[1, snap, field], field, snap)

    def put(index, where, term):
        partial_ref[index, where, :] += term

    def add(snap, carry):
        gather(fields, snap)

        def even_groups(number, inner):
            lag_group(fields, cell_rows, cells // 2, 11 * number - HMAX // 2, 0, 11, put)
            return inner

        def odd_groups(number, inner):
            lag_group(fields, cell_rows, cells // 2, 8 * number - HMAX // 2, 1, 8, put)
            return inner

        lax.fori_loop(0, (HMAX + 1) // 11, even_groups, 0)
        lax.fori_loop(0, HMAX // 8, odd_groups, 0)
        return carry

    lax.fori_loop(0, used - 1, add, 0)
    gather(last_ref, jnp.int32(used - 1))

    for snap in range(used):
        @pl.when(has_right)
        def _():
            up(snap).wait_send()

        @pl.when(has_left)
        def _():
            down(snap).wait_send()


def image_kernel(lags, cell_rows, offset_ref, partial_ref, last_ref, out_ref, image, slot_ref, out_sem):
    cells, cy, nz = out_ref.shape[1:]
    blocks = nz // LANES
    rows = cells * cell_rows

    for index in range(2 * HMAX + 1):
        slot_ref[index] = -1
    for lag in range(lags):
        slot_ref[offset_ref[lag] + HMAX] = lag

    def lanes(block):
        return pl.ds(block * LANES, LANES)

    def put(index, where, term):
        sheet = image.at[index].reshape(rows, LANES)
        sheet[where, :] = partial_ref[index, where, :] + term

    def group(first, odd, width):
        lag_group(last_ref, cell_rows, cells // 2, first, odd, width, put)
        for late in range(width):
            index = 2 * (first + late) + odd + HMAX
            slot = slot_ref[index]

            @pl.when(slot >= 0)
            def _():
                for block in range(blocks):
                    pltpu.make_async_copy(
                        image.at[index, :, block], out_ref.at[slot, :, :, lanes(block)], out_sem).start()

    def even_groups(number, carry):
        group(3 * number - HMAX // 2, 0, 3)
        return carry

    def odd_groups(number, carry):
        group(4 * number - HMAX // 2, 1, 4)
        return carry

    lax.fori_loop(0, (HMAX + 1) // 3, even_groups, 0)
    lax.fori_loop(0, HMAX // 4, odd_groups, 0)
    for block in range(blocks):
        pltpu.make_async_copy(
            image.at[pl.ds(0, lags), :, block], out_ref.at[:, :, :, lanes(block)], out_sem).wait()


def local(tiles, source, receiver, offsets, snap_index):
    stored, cells, cy, nz = source.shape
    used, lags = snap_index.shape[0], offsets.shape[0]
    blocks = nz // LANES
    cell_rows = cy * blocks
    rows = cells * cell_rows
    assert cells == HMAX and (2 * cell_rows) % SUB == 0
    vmem = pl.BlockSpec(memory_space=pltpu.VMEM)
    smem = pl.BlockSpec(memory_space=pltpu.SMEM)
    anywhere = pl.BlockSpec(memory_space=pl.ANY)
    every = 2 * HMAX + 1
    partial, last = pl.pallas_call(
        functools.partial(exchange_kernel, tiles, cell_rows),
        out_shape=(
            jax.ShapeDtypeStruct((every, rows, LANES), jnp.float32),
            jax.ShapeDtypeStruct((2, 3 * rows, LANES), jnp.float32),
        ),
        in_specs=[smem, vmem, vmem],
        out_specs=(vmem, vmem),
        scratch_shapes=[
            pltpu.VMEM((used, 2, cells, blocks, cy, LANES), source.dtype),
            pltpu.VMEM((2, used, 2, cells, blocks, cy, LANES), source.dtype),
            pltpu.VMEM((2, 3 * rows, LANES), jnp.float32),
            pltpu.SemaphoreType.DMA((2, used)),
            pltpu.SemaphoreType.DMA((2, used)),
        ],
        compiler_params=pltpu.CompilerParams(
            collective_id=0, has_side_effects=True, vmem_limit_bytes=32 << 20),
    )(snap_index, source, receiver)
    return pl.pallas_call(
        functools.partial(image_kernel, lags, cell_rows),
        out_shape=jax.ShapeDtypeStruct((lags, cells, cy, nz), jnp.float32),
        in_specs=[smem, vmem, vmem],
        out_specs=anywhere,
        scratch_shapes=[
            pltpu.VMEM((every, cells, blocks, cy, LANES), jnp.float32),
            pltpu.SMEM((every,), jnp.int32),
            pltpu.SemaphoreType.DMA(()),
        ],
        compiler_params=pltpu.CompilerParams(vmem_limit_bytes=32 << 20),
    )(offsets, partial, last)


def solution(mesh):
    return jax.shard_map(
        functools.partial(local, mesh.shape["tile"]),
        mesh=mesh,
        in_specs=(P("shot", "tile", None, None), P("shot", "tile", None, None), P(), P()),
        out_specs=P("shot", "tile", None, None),
        check_vma=False,
    )
```

```python
import functools

import jax
import jax.numpy as jnp
from jax import lax
from jax.experimental import pallas as pl
from jax.experimental.pallas import tpu as pltpu
from jax.sharding import PartitionSpec as P

HMAX = 32
LANES = 128
SUB = 8
MESH = pl.DeviceIdType.MESH


def lag_group(fields, cell_rows, pairs, first, odd, width, put):
    step = 2 * cell_rows
    base = HMAX * cell_rows

    def one_class(part, carry):
        inner = part * SUB
        cache = {}

        def source(place):
            start = base + inner + step * (place - first) - cell_rows * odd
            return fields[0, pl.ds(pl.multiple_of(start, 4), SUB), :]

        def receiver(place):
            if place not in cache:
                start = base + inner + step * (place + first) + cell_rows * odd
                cache[place] = fields[1, pl.ds(pl.multiple_of(start, 4), SUB), :]
            return cache[place]

        for place in range(-(width - 1), pairs):
            held = source(place)
            for late in range(width):
                pair = place + late
                if 0 <= pair < pairs:
                    index = 2 * (first + late) + odd + HMAX
                    rows = pl.ds(pl.multiple_of(step * pair + inner, SUB), SUB)
                    put(index, rows, held * receiver(place + 2 * late))
        return carry

    lax.fori_loop(0, step // SUB, one_class, 0)


def exchange_kernel(
    tiles, cell_rows, snap_ref, src_ref, rec_ref, partial_ref, last_ref,
    picked, halo, fields, send_sem, recv_sem,
):
    me = lax.axis_index("tile")
    has_left, has_right = me > 0, me < tiles - 1
    used, _, cells, blocks, cy, _ = picked.shape
    rows = cells * cell_rows
    barrier = pltpu.get_barrier_semaphore()

    @pl.when(has_left)
    def _():
        pl.semaphore_signal(barrier, inc=1, device_id={"tile": me - 1}, device_id_type=MESH)

    @pl.when(has_right)
    def _():
        pl.semaphore_signal(barrier, inc=1, device_id={"tile": me + 1}, device_id_type=MESH)

    def up(snap):
        return pltpu.make_async_remote_copy(
            src_ref=picked.at[snap],
            dst_ref=halo.at[0, snap],
            send_sem=send_sem.at[0, snap],
            recv_sem=recv_sem.at[0, snap],
            device_id={"tile": me + 1},
            device_id_type=MESH,
        )

    def down(snap):
        return pltpu.make_async_remote_copy(
            src_ref=picked.at[snap],
            dst_ref=halo.at[1, snap],
            send_sem=send_sem.at[1, snap],
            recv_sem=recv_sem.at[1, snap],
            device_id={"tile": me - 1},
            device_id_type=MESH,
        )

    beside = halo.reshape(2, used, 2, rows, LANES)
    own = picked.reshape(used, 2, rows, LANES)
    for snap in range(used):
        for field, ref in enumerate((src_ref, rec_ref)):
            for block in range(blocks):
                picked[snap, field, :, block] = ref[snap_ref[snap], :, :, pl.ds(block * LANES, LANES)]
        if snap == 0:
            pl.semaphore_wait(barrier, has_left.astype(jnp.int32) + has_right.astype(jnp.int32))

        @pl.when(has_right)
        def _():
            up(snap).start()

        @pl.when(has_left)
        def _():
            down(snap).start()

    def clear(place):
        for field in range(2):
            for ref in (fields, last_ref):
                ref[field, pl.ds(place * rows, rows), :] = jnp.zeros((rows, LANES), jnp.float32)

    pl.when(jnp.logical_not(has_left))(functools.partial(clear, 0))
    pl.when(jnp.logical_not(has_right))(functools.partial(clear, 2))

    def zero(index, carry):
        partial_ref[index] = jnp.zeros((rows, LANES), jnp.float32)
        return carry

    lax.fori_loop(0, 2 * HMAX + 1, zero, 0)

    def widen(target, place, value, field, snap):
        value = value.astype(jnp.float32)
        if field == 0:
            value = value * ((snap + 1).astype(jnp.float32) / used)
        target[field, pl.ds(place * rows, rows), :] = value

    def gather(target, snap):
        for field in range(2):
            widen(target, 1, own[snap, field], field, snap)

        @pl.when(has_left)
        def _():
            up(snap).wait_recv()
            for field in range(2):
                widen(target, 0, beside[0, snap, field], field, snap)

        @pl.when(has_right)
        def _():
            down(snap).wait_recv()
            for field in range(2):
                widen(target, 2, beside[1, snap, field], field, snap)

    def put(index, where, term):
        partial_ref[index, where, :] += term

    def add(snap, carry):
        gather(fields, snap)

        def even_groups(number, inner):
            lag_group(fields, cell_rows, cells // 2, 11 * number - HMAX // 2, 0, 11, put)
            return inner

        def odd_groups(number, inner):
            lag_group(fields, cell_rows, cells // 2, 8 * number - HMAX // 2, 1, 8, put)
            return inner

        lax.fori_loop(0, (HMAX + 1) // 11, even_groups, 0)
        lax.fori_loop(0, HMAX // 8, odd_groups, 0)
        return carry

    lax.fori_loop(0, used - 1, add, 0)
    gather(last_ref, jnp.int32(used - 1))

    for snap in range(used):
        @pl.when(has_right)
        def _():
            up(snap).wait_send()

        @pl.when(has_left)
        def _():
            down(snap).wait_send()


def image_kernel(lags, cell_rows, offset_ref, partial_ref, last_ref, out_ref, image, slot_ref, out_sem):
    cells, cy, nz = out_ref.shape[1:]
    blocks = nz // LANES
    rows = cells * cell_rows

    for index in range(2 * HMAX + 1):
        slot_ref[index] = -1
    for lag in range(lags):
        slot_ref[offset_ref[lag] + HMAX] = lag

    def lanes(block):
        return pl.ds(block * LANES, LANES)

    def put(index, where, term):
        sheet = image.at[index].reshape(rows, LANES)
        sheet[where, :] = partial_ref[index, where, :] + term

    def group(first, odd, width):
        lag_group(last_ref, cell_rows, cells // 2, first, odd, width, put)
        for late in range(width):
            index = 2 * (first + late) + odd + HMAX
            slot = slot_ref[index]

            @pl.when(slot >= 0)
            def _():
                for block in range(blocks):
                    pltpu.make_async_copy(
                        image.at[index, :, block], out_ref.at[slot, :, :, lanes(block)], out_sem).start()

    def even_groups(number, carry):
        group(11 * number - HMAX // 2, 0, 11)
        return carry

    def odd_groups(number, carry):
        group(4 * number - HMAX // 2, 1, 4)
        return carry

    lax.fori_loop(0, (HMAX + 1) // 11, even_groups, 0)
    lax.fori_loop(0, HMAX // 4, odd_groups, 0)
    for block in range(blocks):
        pltpu.make_async_copy(
            image.at[pl.ds(0, lags), :, block], out_ref.at[:, :, :, lanes(block)], out_sem).wait()


def local(tiles, source, receiver, offsets, snap_index):
    stored, cells, cy, nz = source.shape
    used, lags = snap_index.shape[0], offsets.shape[0]
    blocks = nz // LANES
    cell_rows = cy * blocks
    rows = cells * cell_rows
    assert cells == HMAX and (2 * cell_rows) % SUB == 0
    vmem = pl.BlockSpec(memory_space=pltpu.VMEM)
    smem = pl.BlockSpec(memory_space=pltpu.SMEM)
    anywhere = pl.BlockSpec(memory_space=pl.ANY)
    every = 2 * HMAX + 1
    partial, last = pl.pallas_call(
        functools.partial(exchange_kernel, tiles, cell_rows),
        out_shape=(
            jax.ShapeDtypeStruct((every, rows, LANES), jnp.float32),
            jax.ShapeDtypeStruct((2, 3 * rows, LANES), jnp.float32),
        ),
        in_specs=[smem, vmem, vmem],
        out_specs=(vmem, vmem),
        scratch_shapes=[
            pltpu.VMEM((used, 2, cells, blocks, cy, LANES), source.dtype),
            pltpu.VMEM((2, used, 2, cells, blocks, cy, LANES), source.dtype),
            pltpu.VMEM((2, 3 * rows, LANES), jnp.float32),
            pltpu.SemaphoreType.DMA((2, used)),
            pltpu.SemaphoreType.DMA((2, used)),
        ],
        compiler_params=pltpu.CompilerParams(
            collective_id=0, has_side_effects=True, vmem_limit_bytes=32 << 20),
    )(snap_index, source, receiver)
    return pl.pallas_call(
        functools.partial(image_kernel, lags, cell_rows),
        out_shape=jax.ShapeDtypeStruct((lags, cells, cy, nz), jnp.float32),
        in_specs=[smem, vmem, vmem],
        out_specs=anywhere,
        scratch_shapes=[
            pltpu.VMEM((every, cells, blocks, cy, LANES), jnp.float32),
            pltpu.SMEM((every,), jnp.int32),
            pltpu.SemaphoreType.DMA(()),
        ],
        compiler_params=pltpu.CompilerParams(vmem_limit_bytes=32 << 20),
    )(offsets, partial, last)


def solution(mesh):
    return jax.shard_map(
        functools.partial(local, mesh.shape["tile"]),
        mesh=mesh,
        in_specs=(P("shot", "tile", None, None), P("shot", "tile", None, None), P(), P()),
        out_specs=P("shot", "tile", None, None),
        check_vma=False,
    )
```
